32 devices in a mesh: groups: 2 (over x), ops: 8 (over z, y), sec: 2 (over core).
Axes of the slice: x: 2, y: 2, z: 4, core: 2. Of those that a mesh axis runs over, the one named last changes fastest.
Arguments:
- wavefunction: bfloat16 [256, 8, 4096], P(None, ('groups', 'sec')), parts along dimension 1, may hold values from -6 to 6
- left_env: bfloat16 [128, 4, 256, 256], P(('groups', 'ops'), 'sec'), parts along dimension 0, may hold values from -0.375 to 0.375
- right_env: bfloat16 [128, 4, 256, 256], P(('groups', 'ops'), 'sec'), parts along dimension 0, may hold values from -0.046875 to 0.046875
- left_site_weight: float32 [12, 4, 4], replicated, may hold values from -3 to 3
- w_right: float32 [12, 4, 4], replicated, may hold values from -3 to 3
- term_id: int32 [128], P(('groups', 'ops')), parts along dimension 0, may hold values from 0 to 11
- left_sizes: int32 [8], P('groups'), parts along dimension 0, may hold values from 64 to 256, as said below
- right_sizes: int32 [8], P('groups'), parts along dimension 0, may hold values from 64 to 256, as said below
- sector_order: int32 [8], P('groups'), parts along dimension 0, may hold values from 0 to 3, as said below
Outputs:
- product: bfloat16 [256, 8, 4096], P('ops', ('groups', 'sec')), parts along dimension 1
The draws below stay inside these ranges and needn't reach their ends.
There are 2 independent parts, one for each index of `groups`. The reference program is written for one: setup_inputs(seed, part) draws one part's arguments, and reference() takes and returns one part's arrays. A program takes and returns all parts, laid end to end along the dimension named above; an argument that names none is the same for every part. Nothing has to cross between parts.
Inputs may be any that keep to these rules, and one draw needn't show every extreme that they name: `left_sizes`: some sector of each part has exactly 256 left bond states. `right_sizes`: some sector of each part has exactly 256 right bond states. `sector_order`: a permutation of the sectors.
All inputs are finite; a program needn't handle non-finite values.
Results may differ from the reference program's by a relative error of at most 0.013.
Values may be sent and summed in bfloat16 or wider, within the bound.
A program may use at most 256 MiB of HBM per device.

```python
import jax
import jax.numpy as jnp
from jax import lax

B = 256
P_SIZE = 16
NW = 12
TERMS = 64
S = 4


def draw_left_sizes(key, part):
    key = jax.random.fold_in(key, 11)
    values = jax.random.randint(key, (S,), B // 4, B + 1)
    where_full = jax.random.randint(jax.random.fold_in(key, 5), (), 0, S)
    return values.at[where_full].set(B).astype(jnp.int32)


def draw_right_sizes(key, part):
    key = jax.random.fold_in(key, 23)
    values = jax.random.randint(key, (S,), B // 4, B + 1)
    where_full = jax.random.randint(jax.random.fold_in(key, 9), (), 0, S)
    return values.at[where_full].set(B).astype(jnp.int32)


def draw_sector_order(key, part):
    key = jax.random.fold_in(key, 37)
    order = jax.random.permutation(key, jnp.arange(S, dtype=jnp.int32))
    return jnp.roll(order, part % S).astype(jnp.int32)


def plant(array, own_key, least, largest):
    longest = array.shape.index(max(array.shape))
    spots = []
    for shift in (0, 1):
        where = [jax.random.randint(jax.random.fold_in(own_key, axis), (), 0, length) for axis, length in enumerate(array.shape)]
        where[longest] = (where[longest] + shift) % array.shape[longest]
        spots.append(tuple(where))
    return array.at[spots[0]].set(least).at[spots[1]].set(largest)


def level_of(stream_key, shape, cuts, low, high):
    level, own = 1.0, jax.random.fold_in(stream_key, 6)
    for axis_at, shards_of in cuts:
        steps = jnp.exp(jax.random.uniform(jax.random.fold_in(own, axis_at), (shards_of,), jnp.float32, low / len(cuts), high / len(cuts)))
        level = level * jnp.repeat(steps, shape[axis_at] // shards_of).reshape([-1 if axis == axis_at else 1 for axis in range(len(shape))])
    return level


def normal_values(stream_key, shape, width, most, cuts=(), held_as=jnp.bfloat16):
    entries = jax.random.normal(stream_key, shape, jnp.float32) * width
    if len(cuts) > 0:
        entries = level_of(stream_key, shape, cuts, -0.22, 0.18) * entries
    return jnp.clip(entries, min=-most, max=most).astype(held_as)


def setup_inputs(seed: int = 0, part: int = 0) -> dict:
    keys = jax.random.split(jax.random.key(seed), 10)
    part_keys = jax.random.split(jax.random.fold_in(keys[9], part), 10)
    wavefunction = normal_values(part_keys[0], (B, S, P_SIZE * B), 1.0, 6.0, ((1, 2),))
    left_env = normal_values(part_keys[1], (TERMS, S, B, B), B ** -0.5, 0.375, ((0, 8), (1, 2)))
    right_env = normal_values(part_keys[2], (TERMS, S, B, B), (B * TERMS) ** -0.5, 0.046875, ((0, 8), (1, 2)))
    left_site_weight = normal_values(keys[3], (NW, 4, 4), 0.5, 3.0, (), jnp.float32)
    w_right = normal_values(keys[4], (NW, 4, 4), 0.5, 3.0, (), jnp.float32)
    term_id = plant(jax.random.randint(part_keys[5], (TERMS,), 0, NW), jax.random.fold_in(part_keys[5], 1), 0, NW - 1).astype(jnp.int32)
    left_sizes = draw_left_sizes(jax.random.fold_in(jax.random.fold_in(keys[9], part), 71), part)
    right_sizes = draw_right_sizes(jax.random.fold_in(jax.random.fold_in(keys[9], part), 71), part)
    sector_order = draw_sector_order(jax.random.fold_in(jax.random.fold_in(keys[9], part), 71), part)
    return dict(wavefunction=wavefunction, left_env=left_env, right_env=right_env, left_site_weight=left_site_weight, w_right=w_right, term_id=term_id, left_sizes=left_sizes, right_sizes=right_sizes, sector_order=sector_order)


def apply_mask(values, size_left, size_right, row_offset):
    row_count = values.shape[0]
    slots = values.shape[1]
    bond = size_left.shape[0] * 0 + B
    row_index = row_offset + jnp.arange(row_count, dtype=jnp.int32)
    col_index = jnp.arange(bond, dtype=jnp.int32)
    keep_left = row_index[:, None] < size_left[None, :]
    keep_right = col_index[None, :] < size_right[:, None]
    keep = keep_left[:, :, None, None] & keep_right[None, :, None, :]
    shaped = values.reshape(row_count, slots, P_SIZE, bond)
    return jnp.where(keep, shaped, jnp.zeros_like(shaped)).reshape(row_count, slots, P_SIZE * bond)


def mixing(left_operator_list, right_operator_list):
    lookup_table = jnp.einsum('ysz,yxe->ysxze', left_operator_list, right_operator_list)
    return lookup_table.reshape(left_operator_list.shape[0], P_SIZE, P_SIZE)


def reference(wavefunction, left_env, right_env, left_site_weight, w_right, term_id, left_sizes, right_sizes, sector_order):
    size_left = left_sizes[sector_order]
    size_right = right_sizes[sector_order]
    work = apply_mask(wavefunction[:, sector_order, :], size_left, size_right, 0)
    lookup_tables = mixing(left_site_weight[term_id], w_right[term_id])
    work_wide = work.astype(jnp.float32)

    def one_term(total, inputs):
        left_blocks, right_blocks, lookup_table = inputs
        applied = jnp.einsum('klm,mkx->lkx', left_blocks.astype(jnp.float32), work_wide).astype(jnp.bfloat16)
        shaped = applied.astype(jnp.float32).reshape(B, S, P_SIZE, B)
        mixed = jnp.einsum('pq,lkqr->lkpr', lookup_table, shaped, precision=lax.Precision.HIGHEST).astype(jnp.bfloat16)
        term = jnp.einsum('lkpr,krs->lkps', mixed.astype(jnp.float32), right_blocks.astype(jnp.float32))
        return total + term.reshape(B, S, P_SIZE * B), None

    start_total = jnp.zeros((B, S, P_SIZE * B), jnp.float32)
    total, _ = lax.scan(one_term, start_total, (left_env, right_env, lookup_tables))
    return apply_mask(total, size_left, size_right, 0).astype(jnp.bfloat16)
```

```python
import functools

import jax
import jax.numpy as jnp
from jax import lax
from jax.experimental import pallas as pl
from jax.experimental.pallas import tpu as pltpu
from jax.sharding import PartitionSpec as P

MESH = pl.DeviceIdType.MESH
SUB = 16
INNER = 2
CHUNKS = 4


def kernel(
    dims,
    wave,
    left,
    right,
    table,
    order_ref,
    left_size_ref,
    right_size_ref,
    out,
    *scratch,
):
    terms, slots, bond, states, ops = dims
    chunk_bufs = scratch[:CHUNKS]
    (
        left_v,
        right_v,
        kron,
        applied,
        mixed,
        own_part,
        pair_out,
        pair_in,
        line_out,
        line_in,
        wave_local_sem,
        wave_send_sem,
        wave_recv_sem,
        env_sem,
        pair_send_sem,
        pair_recv_sem,
        line_send_sem,
        line_recv_sem,
    ) = scratch[CHUNKS:]
    outer = ops // INNER
    blocks = bond // ops // SUB
    steps = slots * outer
    tile = states * SUB
    wide = states * bond // CHUNKS
    per_chunk = states // CHUNKS

    group = lax.axis_index("groups")
    op = lax.axis_index("ops")
    sec = lax.axis_index("sec")
    far = lax.div(op, INNER)
    near = lax.rem(op, INNER)
    other_sec = 1 - sec
    pair_id = (group, far * INNER + (1 - near), sec)
    sec_id = (group, op, other_sec)

    barrier = pltpu.get_barrier_semaphore()
    pl.semaphore_signal(barrier, inc=1, device_id=sec_id, device_id_type=MESH)
    pl.semaphore_signal(barrier, inc=1, device_id=pair_id, device_id_type=MESH)
    for hop in range(1, outer):
        peer = lax.rem(far + hop, outer) * INNER + near
        pl.semaphore_signal(barrier, inc=1, device_id=(group, peer, sec), device_id_type=MESH)
    pl.semaphore_wait(barrier, outer + 1)

    base = sec * slots
    wave_copies = []
    for c in range(CHUNKS):
        source = wave.at[:, :, pl.ds(c * wide, wide)]
        target = chunk_bufs[c].at[pl.ds(base, slots)]
        sent = pltpu.make_async_remote_copy(
            src_ref=source,
            dst_ref=target,
            send_sem=wave_send_sem.at[c],
            recv_sem=wave_recv_sem.at[c],
            device_id=sec_id,
            device_id_type=MESH,
        )
        sent.start()
        kept = pltpu.make_async_copy(source, target, wave_local_sem.at[c])
        kept.start()
        wave_copies.append((sent, kept))
    left_copy = pltpu.make_async_copy(left, left_v, env_sem.at[0])
    left_copy.start()
    right_copy = pltpu.make_async_copy(right, right_v, env_sem.at[1])
    right_copy.start()

    row = lax.broadcasted_iota(jnp.int32, (tile, tile), 0)
    col = lax.broadcasted_iota(jnp.int32, (tile, tile), 1)
    same = (row & (SUB - 1)) == (col & (SUB - 1))
    row_state = lax.broadcasted_iota(jnp.int32, (tile, states), 0) >> 4
    spread = (row_state == lax.broadcasted_iota(jnp.int32, (tile, states), 1)).astype(jnp.bfloat16)
    col_state = lax.broadcasted_iota(jnp.int32, (states, tile), 1) >> 4
    spread_t = (col_state == lax.broadcasted_iota(jnp.int32, (states, tile), 0)).astype(
        jnp.bfloat16
    )
    for t in range(terms):
        tall = jnp.dot(spread, table[t], preferred_element_type=jnp.float32).astype(jnp.bfloat16)
        full = jnp.dot(tall, spread_t, preferred_element_type=jnp.float32)
        kron[t] = jnp.where(same, full, 0.0).astype(jnp.bfloat16)
    left_copy.wait()
    right_copy.wait()

    mask_row = lax.broadcasted_iota(jnp.int32, (bond, bond), 0)
    mask_col = lax.broadcasted_iota(jnp.int32, (bond, bond), 1)

    def apply_left(k, first):
        sector = order_ref[base + k]
        keep = (mask_row < left_size_ref[sector]) & (mask_col < right_size_ref[sector])
        keep = jnp.where(keep, 1.0, 0.0).astype(jnp.bfloat16)
        for c in range(CHUNKS):

            @pl.when(first)
            def _():
                sent, kept = wave_copies[c]
                kept.wait()
                sent.wait_recv()

            @pl.loop(0, per_chunk)
            def _(i):
                lanes = pl.ds(pl.multiple_of(i * bond, bond), bond)
                block = chunk_bufs[c][sector, :, lanes] * keep
                at = pl.ds(pl.multiple_of((c * per_chunk + i) * SUB, SUB), SUB)
                for t in range(0, terms, 2):
                    lhs = left_v[pl.ds(t, 2), k].reshape(2 * bond, bond)
                    res = jnp.dot(lhs, block, preferred_element_type=jnp.float32)
                    res = res.astype(jnp.bfloat16).reshape(2, bond // SUB, SUB, bond)
                    applied[pl.ds(t, 2), :, at, :] = res

    def rows_for(k, dest):
        for b in range(blocks):
            for t in range(terms):
                res = jnp.dot(
                    kron[t], applied[t, dest * blocks + b], preferred_element_type=jnp.float32
                )
                mixed[pl.ds(b * tile, tile), pl.ds(t * bond, bond)] = res.astype(jnp.bfloat16)
        flat = right_v[:, k].reshape(terms * bond, bond)
        return jnp.dot(mixed[...], flat, preferred_element_type=jnp.float32)

    def pair_copy(i):
        return pltpu.make_async_remote_copy(
            src_ref=pair_out.at[i],
            dst_ref=pair_in.at[i],
            send_sem=pair_send_sem.at[i],
            recv_sem=pair_recv_sem.at[i],
            device_id=pair_id,
            device_id_type=MESH,
        )

    def line_copy(i):
        peer = lax.rem(far + 1 + lax.rem(i, outer), outer) * INNER + near
        return pltpu.make_async_remote_copy(
            src_ref=line_out.at[i],
            dst_ref=line_in.at[i],
            send_sem=line_send_sem.at[i],
            recv_sem=line_recv_sem.at[i],
            device_id=(group, peer, sec),
            device_id_type=MESH,
        )

    def combine(i):
        pair_copy(i).wait_recv()

        @pl.when(lax.rem(i, outer) < outer - 1)
        def _():
            line_out[i] = (own_part[i] + pair_in[i].astype(jnp.float32)).astype(jnp.bfloat16)
            line_copy(i).start()

    def step(i, carry):
        k = lax.div(i, outer)
        j = lax.rem(i, outer)

        @pl.when(j == 0)
        def _():
            apply_left(k, i == 0)

        dest = lax.rem(far + 1 + j, outer) * INNER
        pair_out[i] = rows_for(k, dest + (1 - near)).astype(jnp.bfloat16)
        pair_copy(i).start()
        own_part[i] = rows_for(k, dest + near)

        @pl.when(i >= 1)
        def _():
            combine(i - 1)

        return carry

    lax.fori_loop(0, steps, step, 0)
    combine(steps - 1)

    out_row = lax.broadcasted_iota(jnp.int32, (SUB, bond), 0)
    out_col = lax.broadcasted_iota(jnp.int32, (SUB, bond), 1)
    for k in range(slots):
        mine = k * outer + outer - 1
        for j in range(outer - 1):
            line_copy(k * outer + j).wait_recv()
        sector = order_ref[base + k]
        size_left = left_size_ref[sector]
        size_right = right_size_ref[sector]
        for b in range(blocks):
            keep = (out_row + (op * blocks + b) * SUB < size_left) & (out_col < size_right)
            for p in range(states):
                rows = pl.ds(b * tile + p * SUB, SUB)
                total = own_part[mine, rows] + pair_in[mine, rows].astype(jnp.float32)
                for j in range(outer - 1):
                    total = total + line_in[k * outer + j, rows].astype(jnp.float32)
                out[k, pl.ds(b * SUB, SUB), pl.ds(p * bond, bond)] = jnp.where(
                    keep, total, 0.0
                ).astype(jnp.bfloat16)

    for sent, _ in wave_copies:
        sent.wait_send()

    def drain(i, carry):
        pair_copy(i).wait_send()

        @pl.when(lax.rem(i, outer) < outer - 1)
        def _():
            line_copy(i).wait_send()

        return carry

    lax.fori_loop(0, steps, drain, 0)


def local(
    wavefunction,
    left_env,
    right_env,
    left_site_weight,
    w_right,
    term_id,
    left_sizes,
    right_sizes,
    sector_order,
):
    terms, slots, bond = left_env.shape[0], left_env.shape[1], left_env.shape[2]
    states = wavefunction.shape[2] // bond
    ops = lax.axis_size("ops")
    sectors = slots * lax.axis_size("sec")
    operators = left_site_weight.shape[0]
    picker = (term_id[:, None] == jnp.arange(operators, dtype=jnp.int32)[None, :]).astype(
        jnp.float32
    )
    left_ops = jnp.einsum(
        "tn,nac->tac", picker, left_site_weight, precision=lax.Precision.HIGHEST
    )
    right_ops = jnp.einsum("tn,nbd->tbd", picker, w_right, precision=lax.Precision.HIGHEST)
    table = (
        (left_ops[:, :, None, :, None] * right_ops[:, None, :, None, :])
        .reshape(terms, states, states)
        .astype(jnp.bfloat16)
    )
    wave = jnp.transpose(wavefunction, (1, 0, 2))
    outer = ops // INNER
    steps = slots * outer
    share = bond // ops
    rows = share * states
    bf16 = jnp.bfloat16
    any_spec = pl.BlockSpec(memory_space=pl.ANY)
    vmem_spec = pl.BlockSpec(memory_space=pltpu.VMEM)
    smem_spec = pl.BlockSpec(memory_space=pltpu.SMEM)
    result = pl.pallas_call(
        functools.partial(kernel, (terms, slots, bond, states, ops)),
        out_shape=jax.ShapeDtypeStruct((slots, share, states * bond), bf16),
        in_specs=[any_spec, any_spec, any_spec, vmem_spec, smem_spec, smem_spec, smem_spec],
        out_specs=vmem_spec,
        scratch_shapes=[
            pltpu.VMEM((sectors, bond, states * bond // CHUNKS), bf16) for _ in range(CHUNKS)
        ]
        + [
            pltpu.VMEM((terms, slots, bond, bond), bf16),
            pltpu.VMEM((terms, slots, bond, bond), bf16),
            pltpu.VMEM((terms, states * SUB, states * SUB), bf16),
            pltpu.VMEM((terms, bond // SUB, states * SUB, bond), bf16),
            pltpu.VMEM((rows, terms * bond), bf16),
            pltpu.VMEM((steps, rows, bond), jnp.float32),
            pltpu.VMEM((steps, rows, bond), bf16),
            pltpu.VMEM((steps, rows, bond), bf16),
            pltpu.VMEM((steps, rows, bond), bf16),
            pltpu.VMEM((steps, rows, bond), bf16),
            pltpu.SemaphoreType.DMA((CHUNKS,)),
            pltpu.SemaphoreType.DMA((CHUNKS,)),
            pltpu.SemaphoreType.DMA((CHUNKS,)),
            pltpu.SemaphoreType.DMA((2,)),
            pltpu.SemaphoreType.DMA((steps,)),
            pltpu.SemaphoreType.DMA((steps,)),
            pltpu.SemaphoreType.DMA((steps,)),
            pltpu.SemaphoreType.DMA((steps,)),
        ],
        compiler_params=pltpu.CompilerParams(
            collective_id=0, has_side_effects=True, vmem_limit_bytes=56 * 1024 * 1024
        ),
        cost_estimate=pl.CostEstimate(
            flops=6 * terms * slots * states * bond**3, bytes_accessed=2**24, transcendentals=0
        ),
    )(wave, left_env, right_env, table, sector_order, left_sizes, right_sizes)
    return jnp.transpose(result, (1, 0, 2))


def solution(mesh):
    return jax.shard_map(
        local,
        mesh=mesh,
        in_specs=(
            P(None, ("groups", "sec"), None),
            P(("groups", "ops"), "sec", None, None),
            P(("groups", "ops"), "sec", None, None),
            P(),
            P(),
            P(("groups", "ops")),
            P("groups"),
            P("groups"),
            P("groups"),
        ),
        out_specs=P("ops", ("groups", "sec"), None),
        check_vma=False,
    )
```

```python
import functools

import jax
import jax.numpy as jnp
from jax import lax
from jax.experimental import pallas as pl
from jax.experimental.pallas import tpu as pltpu
from jax.sharding import PartitionSpec as P

MESH = pl.DeviceIdType.MESH
SUB = 16
INNER = 2
CHUNKS = 4


def kernel(
    dims,
    wave,
    left,
    right,
    left_op,
    right_op,
    term_ref,
    order_ref,
    left_size_ref,
    right_size_ref,
    out,
    *scratch,
):
    terms, slots, bond, states, ops = dims
    chunk_bufs = scratch[:CHUNKS]
    (
        left_v,
        right_v,
        kron,
        work,
        applied,
        mixed,
        own_part,
        pair_out,
        pair_in,
        line_out,
        line_in,
        wave_local_sem,
        wave_send_sem,
        wave_recv_sem,
        env_sem,
        pair_send_sem,
        pair_recv_sem,
        line_send_sem,
        line_recv_sem,
    ) = scratch[CHUNKS:]
    outer = ops // INNER
    blocks = bond // ops // SUB
    steps = slots * outer
    tile = states * SUB
    pair_rows = INNER * blocks * SUB
    wide = states * bond // CHUNKS
    per_chunk = states // CHUNKS

    group = lax.axis_index("groups")
    op = lax.axis_index("ops")
    sec = lax.axis_index("sec")
    far = lax.div(op, INNER)
    near = lax.rem(op, INNER)
    other_sec = 1 - sec
    pair_id = (group, far * INNER + (1 - near), sec)
    sec_id = (group, op, other_sec)

    barrier = pltpu.get_barrier_semaphore()
    pl.semaphore_signal(barrier, inc=1, device_id=sec_id, device_id_type=MESH)
    pl.semaphore_signal(barrier, inc=1, device_id=pair_id, device_id_type=MESH)
    for hop in range(1, outer):
        peer = lax.rem(far + hop, outer) * INNER + near
        pl.semaphore_signal(barrier, inc=1, device_id=(group, peer, sec), device_id_type=MESH)
    pl.semaphore_wait(barrier, outer + 1)

    base = sec * slots
    wave_copies = []
    for c in range(CHUNKS):
        source = wave.at[:, :, pl.ds(c * wide, wide)]
        target = chunk_bufs[c].at[pl.ds(base, slots)]
        sent = pltpu.make_async_remote_copy(
            src_ref=source,
            dst_ref=target,
            send_sem=wave_send_sem.at[c],
            recv_sem=wave_recv_sem.at[c],
            device_id=sec_id,
            device_id_type=MESH,
        )
        sent.start()
        kept = pltpu.make_async_copy(source, target, wave_local_sem.at[c])
        kept.start()
        wave_copies.append((sent, kept))
    left_copy = pltpu.make_async_copy(left, left_v, env_sem.at[0])
    left_copy.start()
    right_copy = pltpu.make_async_copy(right, right_v, env_sem.at[1])
    right_copy.start()

    row = lax.broadcasted_iota(jnp.int32, (tile, tile), 0)
    col = lax.broadcasted_iota(jnp.int32, (tile, tile), 1)
    same = (row & (SUB - 1)) == (col & (SUB - 1))
    row_state = lax.broadcasted_iota(jnp.int32, (tile, states), 0) >> 4
    spread = (row_state == lax.broadcasted_iota(jnp.int32, (tile, states), 1)).astype(jnp.bfloat16)
    col_state = lax.broadcasted_iota(jnp.int32, (states, tile), 1) >> 4
    spread_t = (col_state == lax.broadcasted_iota(jnp.int32, (states, tile), 0)).astype(
        jnp.bfloat16
    )
    side = left_op.shape[1]
    fine = lax.broadcasted_iota(jnp.int32, (states, side), 0)
    which = lax.broadcasted_iota(jnp.int32, (states, side), 1)
    fine_t = lax.broadcasted_iota(jnp.int32, (side, states), 1)
    which_t = lax.broadcasted_iota(jnp.int32, (side, states), 0)

    def widen(small, by_row, by_col):
        rows = by_row.astype(jnp.float32)
        cols = by_col.astype(jnp.float32)
        tall = jnp.dot(
            rows, small, precision=lax.Precision.HIGHEST, preferred_element_type=jnp.float32
        )
        return jnp.dot(
            tall, cols, precision=lax.Precision.HIGHEST, preferred_element_type=jnp.float32
        )

    for t in range(terms):
        index = term_ref[t]
        from_left = widen(left_op[index], (fine >> 2) == which, (fine_t >> 2) == which_t)
        from_right = widen(right_op[index], (fine & 3) == which, (fine_t & 3) == which_t)
        table = (from_left * from_right).astype(jnp.bfloat16)
        tall = jnp.dot(spread, table, preferred_element_type=jnp.float32).astype(jnp.bfloat16)
        full = jnp.dot(tall, spread_t, preferred_element_type=jnp.float32)
        kron[t] = jnp.where(same, full, 0.0).astype(jnp.bfloat16)
    left_copy.wait()
    right_copy.wait()

    mask_row = lax.broadcasted_iota(jnp.int32, (bond, bond), 0)
    mask_col = lax.broadcasted_iota(jnp.int32, (bond, bond), 1)

    def apply_left(k, first, fresh, dest):
        sector = order_ref[base + k]
        at_rows = pl.ds(pl.multiple_of(dest * blocks * SUB, SUB), pair_rows)
        for c in range(CHUNKS):

            @pl.when(first)
            def _():
                sent, kept = wave_copies[c]
                kept.wait()
                sent.wait_recv()

            @pl.when(fresh)
            def _():
                keep = (mask_row < left_size_ref[sector]) & (mask_col < right_size_ref[sector])
                keep = jnp.where(keep, 1.0, 0.0).astype(jnp.bfloat16)
                for i in range(per_chunk):
                    lanes = pl.ds(i * bond, bond)
                    work[c * per_chunk + i] = chunk_bufs[c][sector, :, lanes] * keep

            @pl.loop(c * per_chunk, (c + 1) * per_chunk)
            def _(q):
                lhs = left_v[:, k, at_rows, :].reshape(terms * pair_rows, bond)
                res = jnp.dot(lhs, work[q], preferred_element_type=jnp.float32)
                at = pl.ds(pl.multiple_of(q * SUB, SUB), SUB)
                applied[:, :, at, :] = res.astype(jnp.bfloat16).reshape(
                    terms, INNER * blocks, SUB, bond
                )

    def rows_for(k, half):
        for b in range(blocks):
            for t in range(terms):
                res = jnp.dot(
                    kron[t], applied[t, half * blocks + b], preferred_element_type=jnp.float32
                )
                mixed[pl.ds(b * tile, tile), pl.ds(t * bond, bond)] = res.astype(jnp.bfloat16)
        flat = right_v[:, k].reshape(terms * bond, bond)
        return jnp.dot(mixed[...], flat, preferred_element_type=jnp.float32)

    def pair_copy(i):
        return pltpu.make_async_remote_copy(
            src_ref=pair_out.at[i],
            dst_ref=pair_in.at[i],
            send_sem=pair_send_sem.at[i],
            recv_sem=pair_recv_sem.at[i],
            device_id=pair_id,
            device_id_type=MESH,
        )

    def line_copy(i):
        peer = lax.rem(far + 1 + lax.rem(i, outer), outer) * INNER + near
        return pltpu.make_async_remote_copy(
            src_ref=line_out.at[i],
            dst_ref=line_in.at[i],
            send_sem=line_send_sem.at[i],
            recv_sem=line_recv_sem.at[i],
            device_id=(group, peer, sec),
            device_id_type=MESH,
        )

    def combine(i):
        pair_copy(i).wait_recv()

        @pl.when(lax.rem(i, outer) < outer - 1)
        def _():
            line_out[i] = (own_part[i] + pair_in[i].astype(jnp.float32)).astype(jnp.bfloat16)
            line_copy(i).start()

    def step(i, carry):
        k = lax.div(i, outer)
        j = lax.rem(i, outer)

        apply_left(k, i == 0, j == 0, lax.rem(far + 1 + j, outer) * INNER)
        pair_out[i] = rows_for(k, 1 - near).astype(jnp.bfloat16)
        pair_copy(i).start()
        own_part[i] = rows_for(k, near)

        @pl.when(i >= 1)
        def _():
            combine(i - 1)

        return carry

    lax.fori_loop(0, steps, step, 0)
    combine(steps - 1)

    out_row = lax.broadcasted_iota(jnp.int32, (SUB, bond), 0)
    out_col = lax.broadcasted_iota(jnp.int32, (SUB, bond), 1)
    for k in range(slots):
        mine = k * outer + outer - 1
        for j in range(outer - 1):
            line_copy(k * outer + j).wait_recv()
        sector = order_ref[base + k]
        size_left = left_size_ref[sector]
        size_right = right_size_ref[sector]
        for b in range(blocks):
            keep = (out_row + (op * blocks + b) * SUB < size_left) & (out_col < size_right)
            for p in range(states):
                rows = pl.ds(b * tile + p * SUB, SUB)
                total = own_part[mine, rows] + pair_in[mine, rows].astype(jnp.float32)
                for j in range(outer - 1):
                    total = total + line_in[k * outer + j, rows].astype(jnp.float32)
                out[k, pl.ds(b * SUB, SUB), pl.ds(p * bond, bond)] = jnp.where(
                    keep, total, 0.0
                ).astype(jnp.bfloat16)

    for sent, _ in wave_copies:
        sent.wait_send()

    def drain(i, carry):
        pair_copy(i).wait_send()

        @pl.when(lax.rem(i, outer) < outer - 1)
        def _():
            line_copy(i).wait_send()

        return carry

    lax.fori_loop(0, steps, drain, 0)


def local(
    wavefunction,
    left_env,
    right_env,
    left_site_weight,
    w_right,
    term_id,
    left_sizes,
    right_sizes,
    sector_order,
):
    terms, slots, bond = left_env.shape[0], left_env.shape[1], left_env.shape[2]
    states = wavefunction.shape[2] // bond
    ops = lax.axis_size("ops")
    sectors = slots * lax.axis_size("sec")
    wave = jnp.transpose(wavefunction, (1, 0, 2))
    outer = ops // INNER
    steps = slots * outer
    share = bond // ops
    rows = share * states
    bf16 = jnp.bfloat16
    any_spec = pl.BlockSpec(memory_space=pl.ANY)
    vmem_spec = pl.BlockSpec(memory_space=pltpu.VMEM)
    smem_spec = pl.BlockSpec(memory_space=pltpu.SMEM)
    result = pl.pallas_call(
        functools.partial(kernel, (terms, slots, bond, states, ops)),
        out_shape=jax.ShapeDtypeStruct((slots, share, states * bond), bf16),
        in_specs=[any_spec] * 3 + [vmem_spec] * 2 + [smem_spec] * 4,
        out_specs=vmem_spec,
        scratch_shapes=[
            pltpu.VMEM((sectors, bond, states * bond // CHUNKS), bf16) for _ in range(CHUNKS)
        ]
        + [
            pltpu.VMEM((terms, slots, bond, bond), bf16),
            pltpu.VMEM((terms, slots, bond, bond), bf16),
            pltpu.VMEM((terms, states * SUB, states * SUB), bf16),
            pltpu.VMEM((states, bond, bond), bf16),
            pltpu.VMEM((terms, INNER * share // SUB, states * SUB, bond), bf16),
            pltpu.VMEM((rows, terms * bond), bf16),
            pltpu.VMEM((steps, rows, bond), jnp.float32),
            pltpu.VMEM((steps, rows, bond), bf16),
            pltpu.VMEM((steps, rows, bond), bf16),
            pltpu.VMEM((steps, rows, bond), bf16),
            pltpu.VMEM((steps, rows, bond), bf16),
            pltpu.SemaphoreType.DMA((CHUNKS,)),
            pltpu.SemaphoreType.DMA((CHUNKS,)),
            pltpu.SemaphoreType.DMA((CHUNKS,)),
            pltpu.SemaphoreType.DMA((2,)),
            pltpu.SemaphoreType.DMA((steps,)),
            pltpu.SemaphoreType.DMA((steps,)),
            pltpu.SemaphoreType.DMA((steps,)),
            pltpu.SemaphoreType.DMA((steps,)),
        ],
        compiler_params=pltpu.CompilerParams(
            collective_id=0, has_side_effects=True, vmem_limit_bytes=56 * 1024 * 1024
        ),
        cost_estimate=pl.CostEstimate(
            flops=6 * terms * slots * states * bond**3, bytes_accessed=2**24, transcendentals=0
        ),
    )(
        wave,
        left_env,
        right_env,
        left_site_weight,
        w_right,
        term_id,
        sector_order,
        left_sizes,
        right_sizes,
    )
    return jnp.transpose(result, (1, 0, 2))


def solution(mesh):
    return jax.shard_map(
        local,
        mesh=mesh,
        in_specs=(
            P(None, ("groups", "sec"), None),
            P(("groups", "ops"), "sec", None, None),
            P(("groups", "ops"), "sec", None, None),
            P(),
            P(),
            P(("groups", "ops")),
            P("groups"),
            P("groups"),
            P("groups"),
        ),
        out_specs=P("ops", ("groups", "sec"), None),
        check_vma=False,
    )
```

```python
import functools

import jax
import jax.numpy as jnp
from jax import lax
from jax.experimental import pallas as pl
from jax.experimental.pallas import tpu as pltpu
from jax.sharding import PartitionSpec as P

MESH = pl.DeviceIdType.MESH
SUB = 16
INNER = 2
CHUNKS = 4


def kernel(
    dims,
    wave,
    left,
    right,
    table,
    order_ref,
    left_size_ref,
    right_size_ref,
    out,
    *scratch,
):
    terms, slots, bond, states, ops = dims
    chunk_bufs = scratch[:CHUNKS]
    (
        left_v,
        right_v,
        kron,
        applied,
        mixed,
        own_part,
        pair_out,
        pair_in,
        line_out,
        line_in,
        wave_local_sem,
        wave_send_sem,
        wave_recv_sem,
        env_sem,
        pair_send_sem,
        pair_recv_sem,
        line_send_sem,
        line_recv_sem,
    ) = scratch[CHUNKS:]
    outer = ops // INNER
    blocks = bond // ops // SUB
    steps = slots * outer
    tile = states * SUB
    wide = states * bond // CHUNKS
    per_chunk = states // CHUNKS

    group = lax.axis_index("groups")
    op = lax.axis_index("ops")
    sec = lax.axis_index("sec")
    far = lax.div(op, INNER)
    near = lax.rem(op, INNER)
    other_sec = 1 - sec
    pair_id = (group, far * INNER + (1 - near), sec)
    sec_id = (group, op, other_sec)

    barrier = pltpu.get_barrier_semaphore()
    pl.semaphore_signal(barrier, inc=1, device_id=sec_id, device_id_type=MESH)
    pl.semaphore_signal(barrier, inc=1, device_id=pair_id, device_id_type=MESH)
    for hop in range(1, outer):
        peer = lax.rem(far + hop, outer) * INNER + near
        pl.semaphore_signal(barrier, inc=1, device_id=(group, peer, sec), device_id_type=MESH)
    pl.semaphore_wait(barrier, outer + 1)

    base = sec * slots
    wave_copies = []
    for c in range(CHUNKS):
        source = wave.at[:, :, pl.ds(c * wide, wide)]
        target = chunk_bufs[c].at[pl.ds(base, slots)]
        sent = pltpu.make_async_remote_copy(
            src_ref=source,
            dst_ref=target,
            send_sem=wave_send_sem.at[c],
            recv_sem=wave_recv_sem.at[c],
            device_id=sec_id,
            device_id_type=MESH,
        )
        sent.start()
        kept = pltpu.make_async_copy(source, target, wave_local_sem.at[c])
        kept.start()
        wave_copies.append((sent, kept))
    left_copy = pltpu.make_async_copy(left, left_v, env_sem.at[0])
    left_copy.start()
    right_copy = pltpu.make_async_copy(right, right_v, env_sem.at[1])
    right_copy.start()

    row = lax.broadcasted_iota(jnp.int32, (tile, tile), 0)
    col = lax.broadcasted_iota(jnp.int32, (tile, tile), 1)
    same = (row & (SUB - 1)) == (col & (SUB - 1))
    row_state = lax.broadcasted_iota(jnp.int32, (tile, states), 0) >> 4
    spread = (row_state == lax.broadcasted_iota(jnp.int32, (tile, states), 1)).astype(jnp.bfloat16)
    col_state = lax.broadcasted_iota(jnp.int32, (states, tile), 1) >> 4
    spread_t = (col_state == lax.broadcasted_iota(jnp.int32, (states, tile), 0)).astype(
        jnp.bfloat16
    )
    for t in range(terms):
        tall = jnp.dot(spread, table[t], preferred_element_type=jnp.float32).astype(jnp.bfloat16)
        full = jnp.dot(tall, spread_t, preferred_element_type=jnp.float32)
        kron[t] = jnp.where(same, full, 0.0).astype(jnp.bfloat16)
    left_copy.wait()
    right_copy.wait()

    mask_row = lax.broadcasted_iota(jnp.int32, (bond, bond), 0)
    mask_col = lax.broadcasted_iota(jnp.int32, (bond, bond), 1)

    def apply_left(k, first):
        sector = order_ref[base + k]
        keep = (mask_row < left_size_ref[sector]) & (mask_col < right_size_ref[sector])
        keep = jnp.where(keep, 1.0, 0.0).astype(jnp.bfloat16)
        for c in range(CHUNKS):

            @pl.when(first)
            def _():
                sent, kept = wave_copies[c]
                kept.wait()
                sent.wait_recv()

            @pl.loop(0, per_chunk)
            def _(i):
                lanes = pl.ds(pl.multiple_of(i * bond, bond), bond)
                block = chunk_bufs[c][sector, :, lanes] * keep
                at = pl.ds(pl.multiple_of((c * per_chunk + i) * SUB, SUB), SUB)
                for t in range(0, terms, 2):
                    lhs = left_v[pl.ds(t, 2), k].reshape(2 * bond, bond)
                    res = jnp.dot(lhs, block, preferred_element_type=jnp.float32)
                    res = res.astype(jnp.bfloat16).reshape(2, bond // SUB, SUB, bond)
                    applied[pl.ds(t, 2), :, at, :] = res

    def rows_for(k, dest):
        for b in range(blocks):
            for t in range(terms):
                res = jnp.dot(
                    kron[t], applied[t, dest * blocks + b], preferred_element_type=jnp.float32
                )
                mixed[pl.ds(b * tile, tile), pl.ds(t * bond, bond)] = res.astype(jnp.bfloat16)
        flat = right_v[:, k].reshape(terms * bond, bond)
        return jnp.dot(mixed[...], flat, preferred_element_type=jnp.float32)

    def pair_copy(i):
        return pltpu.make_async_remote_copy(
            src_ref=pair_out.at[i],
            dst_ref=pair_in.at[i],
            send_sem=pair_send_sem.at[i],
            recv_sem=pair_recv_sem.at[i],
            device_id=pair_id,
            device_id_type=MESH,
        )

    def line_copy(i):
        peer = lax.rem(far + 1 + lax.rem(i, outer), outer) * INNER + near
        return pltpu.make_async_remote_copy(
            src_ref=line_out.at[i],
            dst_ref=line_in.at[i],
            send_sem=line_send_sem.at[i],
            recv_sem=line_recv_sem.at[i],
            device_id=(group, peer, sec),
            device_id_type=MESH,
        )

    def combine(i):
        pair_copy(i).wait_recv()

        @pl.when(lax.rem(i, outer) < outer - 1)
        def _():
            line_out[i] = (own_part[i] + pair_in[i].astype(jnp.float32)).astype(jnp.bfloat16)
            line_copy(i).start()

    def add_lines(k):
        mine = k * outer + outer - 1
        for j in range(outer - 1):
            line_copy(k * outer + j).wait_recv()
        total = own_part[mine]
        for j in range(outer - 1):
            total = total + line_in[k * outer + j].astype(jnp.float32)
        own_part[mine] = total

    out_row = lax.broadcasted_iota(jnp.int32, (SUB, bond), 0)
    out_col = lax.broadcasted_iota(jnp.int32, (SUB, bond), 1)

    def finish(k):
        mine = k * outer + outer - 1
        sector = order_ref[base + k]
        size_left = left_size_ref[sector]
        size_right = right_size_ref[sector]
        for b in range(blocks):
            keep = (out_row + (op * blocks + b) * SUB < size_left) & (out_col < size_right)
            for p in range(states):
                rows = pl.ds(b * tile + p * SUB, SUB)
                total = own_part[mine, rows] + pair_in[mine, rows].astype(jnp.float32)
                out[k, pl.ds(b * SUB, SUB), pl.ds(p * bond, bond)] = jnp.where(
                    keep, total, 0.0
                ).astype(jnp.bfloat16)

    def step(i, carry):
        k = lax.div(i, outer)
        j = lax.rem(i, outer)

        @pl.when(j == 0)
        def _():
            apply_left(k, i == 0)

        dest = lax.rem(far + 1 + j, outer) * INNER
        pair_out[i] = rows_for(k, dest + (1 - near)).astype(jnp.bfloat16)
        pair_copy(i).start()
        own_part[i] = rows_for(k, dest + near)

        @pl.when(i >= 1)
        def _():
            combine(i - 1)

        for done in range(slots - 1):

            @pl.when(i == (done + 1) * outer + min(2, outer - 1))
            def _():
                add_lines(done)
                finish(done)

        return carry

    lax.fori_loop(0, steps, step, 0)
    add_lines(slots - 1)
    combine(steps - 1)
    finish(slots - 1)

    for sent, _ in wave_copies:
        sent.wait_send()

    def drain(i, carry):
        pair_copy(i).wait_send()

        @pl.when(lax.rem(i, outer) < outer - 1)
        def _():
            line_copy(i).wait_send()

        return carry

    lax.fori_loop(0, steps, drain, 0)


def local(
    wavefunction,
    left_env,
    right_env,
    left_site_weight,
    w_right,
    term_id,
    left_sizes,
    right_sizes,
    sector_order,
):
    terms, slots, bond = left_env.shape[0], left_env.shape[1], left_env.shape[2]
    states = wavefunction.shape[2] // bond
    ops = lax.axis_size("ops")
    sectors = slots * lax.axis_size("sec")
    operators = left_site_weight.shape[0]
    picker = (term_id[:, None] == jnp.arange(operators, dtype=jnp.int32)[None, :]).astype(
        jnp.float32
    )
    left_ops = jnp.einsum(
        "tn,nac->tac", picker, left_site_weight, precision=lax.Precision.HIGHEST
    )
    right_ops = jnp.einsum("tn,nbd->tbd", picker, w_right, precision=lax.Precision.HIGHEST)
    table = (
        (left_ops[:, :, None, :, None] * right_ops[:, None, :, None, :])
        .reshape(terms, states, states)
        .astype(jnp.bfloat16)
    )
    wave = jnp.transpose(wavefunction, (1, 0, 2))
    outer = ops // INNER
    steps = slots * outer
    share = bond // ops
    rows = share * states
    bf16 = jnp.bfloat16
    any_spec = pl.BlockSpec(memory_space=pl.ANY)
    vmem_spec = pl.BlockSpec(memory_space=pltpu.VMEM)
    smem_spec = pl.BlockSpec(memory_space=pltpu.SMEM)
    result = pl.pallas_call(
        functools.partial(kernel, (terms, slots, bond, states, ops)),
        out_shape=jax.ShapeDtypeStruct((slots, share, states * bond), bf16),
        in_specs=[any_spec, any_spec, any_spec, vmem_spec, smem_spec, smem_spec, smem_spec],
        out_specs=vmem_spec,
        scratch_shapes=[
            pltpu.VMEM((sectors, bond, states * bond // CHUNKS), bf16) for _ in range(CHUNKS)
        ]
        + [
            pltpu.VMEM((terms, slots, bond, bond), bf16),
            pltpu.VMEM((terms, slots, bond, bond), bf16),
            pltpu.VMEM((terms, states * SUB, states * SUB), bf16),
            pltpu.VMEM((terms, bond // SUB, states * SUB, bond), bf16),
            pltpu.VMEM((rows, terms * bond), bf16),
            pltpu.VMEM((steps, rows, bond), jnp.float32),
            pltpu.VMEM((steps, rows, bond), bf16),
            pltpu.VMEM((steps, rows, bond), bf16),
            pltpu.VMEM((steps, rows, bond), bf16),
            pltpu.VMEM((steps, rows, bond), bf16),
            pltpu.SemaphoreType.DMA((CHUNKS,)),
            pltpu.SemaphoreType.DMA((CHUNKS,)),
            pltpu.SemaphoreType.DMA((CHUNKS,)),
            pltpu.SemaphoreType.DMA((2,)),
            pltpu.SemaphoreType.DMA((steps,)),
            pltpu.SemaphoreType.DMA((steps,)),
            pltpu.SemaphoreType.DMA((steps,)),
            pltpu.SemaphoreType.DMA((steps,)),
        ],
        compiler_params=pltpu.CompilerParams(
            collective_id=0, has_side_effects=True, vmem_limit_bytes=56 * 1024 * 1024
        ),
        cost_estimate=pl.CostEstimate(
            flops=6 * terms * slots * states * bond**3, bytes_accessed=2**24, transcendentals=0
        ),
    )(wave, left_env, right_env, table, sector_order, left_sizes, right_sizes)
    return jnp.transpose(result, (1, 0, 2))


def solution(mesh):
    return jax.shard_map(
        local,
        mesh=mesh,
        in_specs=(
            P(None, ("groups", "sec"), None),
            P(("groups", "ops"), "sec", None, None),
            P(("groups", "ops"), "sec", None, None),
            P(),
            P(),
            P(("groups", "ops")),
            P("groups"),
            P("groups"),
            P("groups"),
        ),
        out_specs=P("ops", ("groups", "sec"), None),
        check_vma=False,
    )
```
